32 devices in a mesh: parts: 2 (over y), row: 4 (over z), col: 2 (over x), chan: 2 (over core).
Axes of the slice: x: 2, y: 2, z: 4, core: 2. Of those that a mesh axis runs over, the one named last changes fastest.
Arguments:
- pair_state: float32 [192, 96, 128], P(('parts', 'row'), 'col'), parts along dimension 0, may hold values from -30 to 30
- input_weights: bfloat16 [2, 128, 4, 128], replicated, may hold values from -0.5 to 0.5
- gate_weights: bfloat16 [2, 128, 128], replicated, may hold values from -0.5 to 0.5
- output_weights: bfloat16 [2, 128, 128], replicated, may hold values from -0.5 to 0.5
Outputs:
- updated_pair: float32 [192, 96, 128], P(('parts', 'row'), 'col'), parts along dimension 0
The draws below stay inside these ranges and needn't reach their ends.
There are 2 independent parts, one for each index of `parts`. The reference program is written for one: setup_inputs(seed, part) draws one part's arguments, and reference() takes and returns one part's arrays. A program takes and returns all parts, laid end to end along the dimension named above; an argument that names none is the same for every part. Nothing has to cross between parts.
All inputs are finite; a program needn't handle non-finite values.
Results may differ from the reference program's by a relative error of at most 0.0028.
Values may be sent and summed in bfloat16 or wider, within the bound.
A program may use at most 64 MiB of HBM per device.

```python
import math
import jax
import jax.numpy as jnp
from jax import lax

C = 128
H = 128
N = 96


def draw_pair_state(key, part):
    key = jax.random.fold_in(key, 11)
    keys = jax.random.split(key, 3)
    base = jax.random.truncated_normal(keys[0], -3.0, 3.0, (N, N, C), jnp.float32)
    cells = jnp.exp(jax.random.uniform(keys[1], (N, N, 1), jnp.float32, math.log(0.3), math.log(3.0)))
    channels = jnp.exp(jax.random.uniform(keys[2], (C,), jnp.float32, math.log(0.3), math.log(3.0)))
    return base * cells * channels


def bell_draw(rng, shape, spread, bound, held_as=jnp.bfloat16):
    entries = spread * jax.random.normal(rng, shape, jnp.float32)
    return jnp.clip(entries, min=-bound, max=bound).astype(held_as)


def setup_inputs(seed: int = 0, part: int = 0) -> dict:
    key_of = jax.random.split(jax.random.key(seed), 5)
    part_splits = jax.random.split(jax.random.fold_in(key_of[4], part), 5)
    pair_state = draw_pair_state(jax.random.fold_in(jax.random.fold_in(key_of[4], part), 71), part)
    input_weights = bell_draw(key_of[1], (2, C, 4, H), C ** -0.5, 0.5)
    gate_weights = bell_draw(key_of[2], (2, C, C), C ** -0.5, 0.5)
    output_weights = bell_draw(key_of[3], (2, H, C), H ** -0.5, 0.5)
    return {"pair_state": pair_state, "input_weights": input_weights, "gate_weights": gate_weights, "output_weights": output_weights}


EPSILON = 1e-05

def normalize(values, hidden_axis):
    average = lax.optimization_barrier(jnp.mean(values, axis=hidden_axis, keepdims=True))
    centered = values - average
    variance = lax.optimization_barrier(jnp.mean(centered * centered, axis=hidden_axis, keepdims=True))
    return centered * lax.rsqrt(variance + EPSILON)

def triangle(state, weights_in, weights_gate, weights_out, form):
    normed = lax.optimization_barrier(normalize(state, 2).astype(jnp.bfloat16)).astype(jnp.float32)
    projected = jnp.einsum('ijc,cgh->ghij', normed, weights_in.astype(jnp.float32))
    left_panel = lax.optimization_barrier((jax.nn.sigmoid(projected[0]) * projected[1]).astype(jnp.bfloat16))
    right_panel = lax.optimization_barrier((jax.nn.sigmoid(projected[2]) * projected[3]).astype(jnp.bfloat16))
    gating = jax.nn.sigmoid(jnp.einsum('ijc,cd->ijd', normed, weights_gate.astype(jnp.float32)))
    mixed = jnp.einsum(form, left_panel.astype(jnp.float32), right_panel.astype(jnp.float32))
    scaled = lax.optimization_barrier(normalize(mixed, 2).astype(jnp.bfloat16)).astype(jnp.float32)
    return state + gating * jnp.einsum('ijh,hc->ijc', scaled, weights_out.astype(jnp.float32))

def reference(pair_state, input_weights, gate_weights, output_weights):
    state = triangle(pair_state, input_weights[0], gate_weights[0], output_weights[0], 'hik,hjk->ijh')
    state = triangle(state, input_weights[1], gate_weights[1], output_weights[1], 'hki,hkj->ijh')
    return state
```

```python
import functools

import jax
import jax.numpy as jnp
from jax import lax
from jax.experimental import pallas as pl
from jax.experimental.pallas import tpu as pltpu
from jax.sharding import PartitionSpec as P

EPSILON = 1e-05
MESH = pl.DeviceIdType.MESH
BF16, F32 = jnp.bfloat16, jnp.float32


def normalize(values):
    average = jnp.mean(values, axis=-1, keepdims=True)
    centered = values - average
    variance = jnp.mean(centered * centered, axis=-1, keepdims=True)
    return centered * lax.rsqrt(variance + EPSILON)


def sigmoid(v):
    return jax.nn.sigmoid(v)


def triangle(left_row, right_slab, depth, columns, block=8):
    def step(k, sums):
        right = right_slab(k)
        return tuple(sums[i] + left_row(k, i) * right for i in range(block))

    zero = jnp.zeros((columns, 128), F32)
    return lax.fori_loop(0, depth, step, (zero,) * block, unroll=4)


def kernel(
    n_row, n_col, state_ref, w_in_ref, w_gate_ref, w_out_ref, out_ref,
    cells, turned, gating, mixed,
    left_own, left_mate, left_full, right_own, right_got, right_full,
    part0_send, part0_got,
    left1_got, left1_full, right1_full, part1_send, part1_got,
    l_send, l_recv, r_send, r_recv, p0_send, p0_recv,
    l1_send, l1_recv, p1_send, p1_recv, o_send, o_recv,
):
    r, c, ch = lax.axis_index("row"), lax.axis_index("col"), lax.axis_index("chan")
    mate = 1 - ch
    rb = state_ref.shape[0]
    cb = state_ref.shape[1] // 2
    total = rb * cb
    q = cb // rb
    chunk = 96 if total % 96 == 0 else total
    mine = pl.multiple_of(ch * cb, 8)
    other = pl.multiple_of(mate * cb, 8)
    tile = 2 * c + ch

    def at(row, col, chan):
        return {"row": row, "col": col, "chan": chan}

    barrier = pltpu.get_barrier_semaphore()
    greeted = 0
    for dr in range(n_row):
        for dch in range(2):
            if dr or dch:
                pl.semaphore_signal(
                    barrier, inc=1, device_id=at(lax.rem(r + dr, n_row), c, lax.rem(ch + dch, 2)), device_id_type=MESH
                )
                greeted += 1
    for dc in range(1, n_col):
        for dch in range(2):
            pl.semaphore_signal(
                barrier, inc=1, device_id=at(r, lax.rem(c + dc, n_col), lax.rem(ch + dch, 2)), device_id_type=MESH
            )
            greeted += 1

    def rows_of(step):
        return pl.ds(pl.multiple_of(step * chunk, 32), chunk)

    def panel(normed, u, side):
        both = jnp.dot(normed, w_in_ref[u, side], preferred_element_type=F32)
        return (sigmoid(both[:, :128]) * both[:, 128:]).astype(BF16)

    cells[...] = state_ref[:, pl.ds(mine, cb), :].reshape(total, 128)

    def turn(k, _):
        turned[pl.ds(pl.multiple_of(k * rb, 8), rb), :] = cells[pl.ds(k, rb, stride=cb), :]
        return 0

    lax.fori_loop(0, cb, turn, 0)

    def project_right(step, _):
        rows = rows_of(step)
        right_own[rows, :] = panel(normalize(turned[rows, :]).astype(BF16), 0, 1)
        return 0

    lax.fori_loop(0, total // chunk, project_right, 0)

    pl.semaphore_wait(barrier, greeted)

    aim = lax.rem(r // q, 2)
    slot = (r // q) // 2 * q + lax.rem(r, q)

    def right_copy(row, chan, index):
        return pltpu.make_async_remote_copy(
            src_ref=right_own, dst_ref=right_got.at[slot, ch], send_sem=r_send.at[index],
            recv_sem=r_recv.at[slot, ch], device_id=at(row, c, chan), device_id_type=MESH,
        )

    for d in range(1, n_row):
        right_copy(lax.rem(r + d, n_row), aim, d).start()

    @pl.when(aim != ch)
    def _():
        right_copy(r, mate, 0).start()

    @pl.when(aim == ch)
    def _():
        pltpu.make_async_copy(right_own, right_got.at[slot, ch], r_recv.at[slot, ch]).start()

    def project_left(step, _):
        rows = rows_of(step)
        normed = normalize(cells[rows, :]).astype(BF16)
        left_own[rows, :] = panel(normed, 0, 0)
        gating[rows, :] = sigmoid(jnp.dot(normed, w_gate_ref[0], preferred_element_type=F32))
        return 0

    lax.fori_loop(0, total // chunk, project_left, 0)
    left_copy = pltpu.make_async_remote_copy(
        src_ref=left_own, dst_ref=left_mate, send_sem=l_send, recv_sem=l_recv,
        device_id=at(r, c, mate), device_id_type=MESH,
    )
    left_copy.start()
    left_full[:, pl.ds(mine, cb), :] = left_own[...].astype(F32).reshape(rb, cb, 128)
    left_copy.wait_recv()
    left_full[:, pl.ds(other, cb), :] = left_mate[...].astype(F32).reshape(rb, cb, 128)

    def part0_copy(index, col):
        return pltpu.make_async_remote_copy(
            src_ref=part0_send.at[index], dst_ref=part0_got.at[index], send_sem=p0_send.at[index],
            recv_sem=p0_recv.at[index], device_id=at(r, col, ch), device_id_type=MESH,
        )

    for d in range(1, n_col + 1):
        col = lax.rem(c + d, n_col)
        for off in range(q):
            source = col * q + off
            for core in range(2):
                pltpu.make_async_copy(right_own, right_got.at[source, core], r_recv.at[source, core]).wait()
                right_full[core * cb:(core + 1) * cb] = right_got[source, core].astype(F32).reshape(cb, rb, 128)

            def rows_block(b, _):
                sums = triangle(
                    lambda k, i: left_full[b * 8 + i, pl.ds(k, 1), :],
                    lambda k: right_full[k],
                    2 * cb, rb,
                )
                for i in range(8):
                    mixed[b * 8 + i, off * rb:(off + 1) * rb, :] = sums[i]
                return 0

            lax.fori_loop(0, rb // 8, rows_block, 0)
        if d < n_col:
            part0_send[d - 1] = mixed[...].reshape(total, 128).astype(BF16)
            part0_copy(d - 1, col).start()
    for d in range(1, n_col):
        part0_copy(d - 1, lax.rem(c + d, n_col)).wait_recv()

    def finish(u, got, count, total_sums):
        turned[...] = total_sums

        def step(s, _):
            rows = rows_of(s)
            values = turned[rows, :]
            for index in range(count):
                values += got[index, rows, :].astype(F32)
            scaled = normalize(values).astype(BF16)
            grown = jnp.dot(scaled, w_out_ref[u], preferred_element_type=F32)
            cells[rows, :] = cells[rows, :] + gating[rows, :] * grown
            return 0

        lax.fori_loop(0, total // chunk, step, 0)

    finish(0, part0_got, n_col - 1, mixed[...].reshape(total, 128))

    def project_left1(step, _):
        rows = rows_of(step)
        left1_got[tile, rows, :] = panel(normalize(cells[rows, :]).astype(BF16), 1, 0)
        return 0

    lax.fori_loop(0, total // chunk, project_left1, 0)

    peers = [(lax.rem(c + dc, n_col), lax.rem(ch + dch, 2)) for dc in range(n_col) for dch in range(2)][1:]

    def left1_copy(index):
        col, chan = peers[index]
        return pltpu.make_async_remote_copy(
            src_ref=left1_got.at[tile], dst_ref=left1_got.at[tile], send_sem=l1_send.at[index],
            recv_sem=l1_recv.at[tile], device_id=at(r, col, chan), device_id_type=MESH,
        )

    for index in range(len(peers)):
        left1_copy(index).start()

    def project_rest(step, _):
        rows = rows_of(step)
        normed = normalize(cells[rows, :]).astype(BF16)
        turned[rows, :] = panel(normed, 1, 1).astype(F32)
        gating[rows, :] = sigmoid(jnp.dot(normed, w_gate_ref[1], preferred_element_type=F32))
        return 0

    lax.fori_loop(0, total // chunk, project_rest, 0)
    right1_full[...] = turned[...].reshape(rb, cb, 128)

    def left1_take(t):
        taken = left1_got[t].astype(F32).reshape(rb, cb, 128)
        for off in range(q):
            left1_full[t * q + off] = taken[:, off * rb:(off + 1) * rb, :]

    left1_take(tile)
    for index, (col, chan) in enumerate(peers):
        t = 2 * col + chan
        pltpu.make_async_remote_copy(
            src_ref=left1_got.at[t], dst_ref=left1_got.at[t], send_sem=l1_send.at[index],
            recv_sem=l1_recv.at[t], device_id=at(r, col, chan), device_id_type=MESH,
        ).wait_recv()
        left1_take(t)

    def part1_copy(index, row):
        return pltpu.make_async_remote_copy(
            src_ref=part1_send.at[index], dst_ref=part1_got.at[index], send_sem=p1_send.at[index],
            recv_sem=p1_recv.at[index], device_id=at(row, c, ch), device_id_type=MESH,
        )

    for d in range(1, n_row + 1):
        row = lax.rem(r + d, n_row)
        for off in range(q):

            def rows_block1(b, _):
                sums = triangle(
                    lambda k, i: left1_full[row, k, pl.ds(b * 8 + i, 1), :],
                    lambda k: right1_full[k, off * rb:(off + 1) * rb, :],
                    rb, rb,
                )
                for i in range(8):
                    mixed[b * 8 + i, off * rb:(off + 1) * rb, :] = sums[i]
                return 0

            lax.fori_loop(0, rb // 8, rows_block1, 0)
        if d < n_row:
            part1_send[d - 1] = mixed[...].reshape(total, 128).astype(BF16)
            part1_copy(d - 1, row).start()
    for d in range(1, n_row):
        part1_copy(d - 1, lax.rem(r + d, n_row)).wait_recv()
    finish(1, part1_got, n_row - 1, mixed[...].reshape(total, 128))

    out_ref[:, pl.ds(mine, cb), :] = cells[...].reshape(rb, cb, 128)
    out_copy = pltpu.make_async_remote_copy(
        src_ref=out_ref.at[:, pl.ds(mine, cb), :], dst_ref=out_ref.at[:, pl.ds(mine, cb), :], send_sem=o_send,
        recv_sem=o_recv, device_id=at(r, c, mate), device_id_type=MESH,
    )
    out_copy.start()

    for d in range(1, n_row):
        right_copy(lax.rem(r + d, n_row), aim, d).wait_send()

    @pl.when(aim != ch)
    def _():
        right_copy(r, mate, 0).wait_send()

    left_copy.wait_send()
    for d in range(1, n_col):
        part0_copy(d - 1, lax.rem(c + d, n_col)).wait_send()
    for index in range(len(peers)):
        left1_copy(index).wait_send()
    for d in range(1, n_row):
        part1_copy(d - 1, lax.rem(r + d, n_row)).wait_send()
    out_copy.wait()


def on_device(n_row, n_col, pair_state, input_weights, gate_weights, output_weights):
    rb, cols, channels = pair_state.shape
    cb = cols // 2
    total, q = rb * cb, cb // rb
    w_in = input_weights.reshape(2, channels, 2, 2 * channels).transpose(0, 2, 1, 3)
    vmem = pl.BlockSpec(memory_space=pltpu.VMEM)
    dma = pltpu.SemaphoreType.DMA
    slots = n_row // 2
    scratch = [
        pltpu.VMEM((total, channels), F32),
        pltpu.VMEM((total, channels), F32),
        pltpu.VMEM((total, channels), F32),
        pltpu.VMEM((rb, cb, channels), F32),
        pltpu.VMEM((total, channels), BF16),
        pltpu.VMEM((total, channels), BF16),
        pltpu.VMEM((rb, 2 * cb, channels), F32),
        pltpu.VMEM((total, channels), BF16),
        pltpu.VMEM((slots, 2, total, channels), BF16),
        pltpu.VMEM((2 * cb, rb, channels), F32),
        pltpu.VMEM((n_col - 1, total, channels), BF16),
        pltpu.VMEM((n_col - 1, total, channels), BF16),
        pltpu.VMEM((2 * n_col, total, channels), BF16),
        pltpu.VMEM((n_row, rb, rb, channels), F32),
        pltpu.VMEM((rb, cb, channels), F32),
        pltpu.VMEM((n_row - 1, total, channels), BF16),
        pltpu.VMEM((n_row - 1, total, channels), BF16),
        dma, dma, dma((n_row,)), dma((slots, 2)), dma((n_col - 1,)), dma((n_col - 1,)),
        dma((2 * n_col - 1,)), dma((2 * n_col,)), dma((n_row - 1,)), dma((n_row - 1,)), dma, dma,
    ]
    return pl.pallas_call(
        functools.partial(kernel, n_row, n_col),
        out_shape=jax.ShapeDtypeStruct(pair_state.shape, F32),
        in_specs=[vmem] * 4,
        out_specs=vmem,
        scratch_shapes=scratch,
        compiler_params=pltpu.CompilerParams(
            collective_id=0, has_side_effects=True, vmem_limit_bytes=50 * 1024 * 1024
        ),
    )(pair_state, w_in, gate_weights, output_weights)


def solution(mesh):
    placed = (P(("parts", "row"), "col", None), P(), P(), P())
    return jax.shard_map(
        functools.partial(on_device, mesh.shape["row"], mesh.shape["col"]),
        mesh=mesh,
        in_specs=placed,
        out_specs=P(("parts", "row"), "col", None),
        check_vma=False,
    )
```

```python
import functools

import jax
import jax.numpy as jnp
from jax import lax
from jax.experimental import pallas as pl
from jax.experimental.pallas import tpu as pltpu
from jax.sharding import PartitionSpec as P

EPSILON = 1e-05
MESH = pl.DeviceIdType.MESH
BF16, F32 = jnp.bfloat16, jnp.float32


def normalize(values):
    average = jnp.mean(values, axis=-1, keepdims=True)
    centered = values - average
    variance = jnp.mean(centered * centered, axis=-1, keepdims=True)
    return centered * lax.rsqrt(variance + EPSILON)


def sigmoid(v):
    return jax.nn.sigmoid(v)


def triangle(left_row, right_slab, depth, columns, block):
    def step(k, sums):
        right = right_slab(k)
        return tuple(sums[i] + left_row(k, i) * right for i in range(block))

    zero = jnp.zeros((columns, 128), F32)
    return lax.fori_loop(0, depth, step, (zero,) * block, unroll=4)


def kernel(
    n_row, n_col, state_ref, w_in_ref, w_gate_ref, w_out_ref, out_ref,
    cells, turned, gating, mixed0,
    left_own, left_mate, left_full, right_own, right_got, right_full,
    part0_send, part0_got,
    left1_got, left1_full, right1_own, right1_mate, right1_full, part1_send, part1_got,
    l_send, l_recv, r_send, r_recv, p0_send, p0_recv,
    l1_send, l1_recv, m_send, m_recv, p1_send, p1_recv, o_send, o_recv,
):
    r, c, ch = lax.axis_index("row"), lax.axis_index("col"), lax.axis_index("chan")
    mate = 1 - ch
    rb = state_ref.shape[0]
    cb = state_ref.shape[1] // 2
    q = cb // rb
    pr, pc = rb // 8, cb // 8
    mine = pl.multiple_of(ch * cb, 8)

    def at(row, col, chan):
        return {"row": row, "col": col, "chan": chan}

    def col_start(core, piece):
        return pl.multiple_of(core * cb + piece * 8, 8)

    barrier = pltpu.get_barrier_semaphore()
    greeted = 0
    for dr in range(n_row):
        for dch in range(2):
            if dr or dch:
                pl.semaphore_signal(
                    barrier, inc=1, device_id=at(lax.rem(r + dr, n_row), c, lax.rem(ch + dch, 2)), device_id_type=MESH
                )
                greeted += 1
    for dc in range(1, n_col):
        pl.semaphore_signal(barrier, inc=1, device_id=at(r, lax.rem(c + dc, n_col), ch), device_id_type=MESH)
        greeted += 1

    def panel(normed, u, side):
        both = jnp.dot(normed, w_in_ref[u, side], preferred_element_type=F32)
        return (sigmoid(both[:, :128]) * both[:, 128:]).astype(BF16)

    def gate(normed, u):
        return sigmoid(jnp.dot(normed, w_gate_ref[u], preferred_element_type=F32))

    def grown(values, u):
        return jnp.dot(normalize(values).astype(BF16), w_out_ref[u], preferred_element_type=F32)

    for p in range(pc):
        cells[p] = state_ref[:, pl.ds(col_start(ch, p), 8), :].reshape(rb * 8, 128)

    aim = lax.rem(r // q, 2)
    slot = (r // q) // 2 * q + lax.rem(r, q)

    def right_copy(row, chan, index, p):
        return pltpu.make_async_remote_copy(
            src_ref=right_own.at[p], dst_ref=right_got.at[slot, ch, p], send_sem=r_send.at[index, p],
            recv_sem=r_recv.at[slot, ch, p], device_id=at(row, c, chan), device_id_type=MESH,
        )

    for p in range(pr):
        for k in range(cb):
            turned[k * 8:(k + 1) * 8, :] = cells[k // 8, pl.ds(p * 64 + k % 8, 8, stride=8), :]
        right_own[p] = panel(normalize(turned[...]).astype(BF16), 0, 1)
        if p == 0:
            pl.semaphore_wait(barrier, greeted)
        for d in range(1, n_row):
            right_copy(lax.rem(r + d, n_row), aim, d, p).start()

        @pl.when(aim != ch)
        def _():
            right_copy(r, mate, 0, p).start()

        @pl.when(aim == ch)
        def _():
            pltpu.make_async_copy(right_own.at[p], right_got.at[slot, ch, p], r_recv.at[slot, ch, p]).start()

    for p in range(pc):
        normed = normalize(cells[p]).astype(BF16)
        left_own[p] = panel(normed, 0, 0)
        gating[p] = gate(normed, 0)
    left_copy = pltpu.make_async_remote_copy(
        src_ref=left_own, dst_ref=left_mate, send_sem=l_send, recv_sem=l_recv,
        device_id=at(r, c, mate), device_id_type=MESH,
    )
    left_copy.start()
    for p in range(pc):
        left_full[:, pl.ds(col_start(ch, p), 8), :] = left_own[p].astype(F32).reshape(rb, 8, 128)
    left_copy.wait_recv()
    for p in range(pc):
        left_full[:, pl.ds(col_start(mate, p), 8), :] = left_mate[p].astype(F32).reshape(rb, 8, 128)

    def part0_copy(d, piece):
        return pltpu.make_async_remote_copy(
            src_ref=part0_send.at[d - 1, piece], dst_ref=part0_got.at[d - 1, piece], send_sem=p0_send.at[d - 1, piece],
            recv_sem=p0_recv.at[d - 1, piece], device_id=at(r, lax.rem(c + d, n_col), ch), device_id_type=MESH,
        )

    def left1_copy(d, t, piece):
        return pltpu.make_async_remote_copy(
            src_ref=left1_got.at[t, piece], dst_ref=left1_got.at[t, piece], send_sem=l1_send.at[d - 1, piece],
            recv_sem=l1_recv.at[t, piece], device_id=at(r, lax.rem(c + d, n_col), ch), device_id_type=MESH,
        )

    def conclude(piece):
        values = mixed0[piece]
        for d in range(1, n_col):
            part0_copy(d, piece).wait_recv()
            values += part0_got[d - 1, piece].astype(F32)
        state = cells[piece] + gating[piece] * grown(values, 0)
        cells[piece] = state
        normed = normalize(state).astype(BF16)
        left1_got[c, piece] = panel(normed, 1, 0)
        for d in range(1, n_col):
            left1_copy(d, c, piece).start()
        right1_own[piece] = panel(normed, 1, 1)
        gating[piece] = gate(normed, 1)

    pieces = [(off, p) for p in range(pr) for off in range(q)]
    for number, (off, p) in enumerate(pieces):
        piece = off * pr + p
        for d in range(1, n_col + 1):
            source = lax.rem(c + d, n_col) * q + off
            for core in range(2):
                pltpu.make_async_copy(
                    right_own.at[p], right_got.at[source, core, p], r_recv.at[source, core, p]
                ).wait()
                right_full[core * cb:(core + 1) * cb] = right_got[source, core, p].astype(F32).reshape(cb, 8, 128)
            sums = triangle(
                lambda k, i: left_full[i, pl.ds(k, 1), :], lambda k: right_full[k], 2 * cb, 8, rb
            )
            if d < n_col:
                part0_send[d - 1, piece] = jnp.stack(sums).reshape(rb * 8, 128).astype(BF16)
                part0_copy(d, piece).start()
            else:
                mixed0[piece] = jnp.stack(sums).reshape(rb * 8, 128)
        if number:
            before = pieces[number - 1]
            conclude(before[0] * pr + before[1])
    conclude(pieces[-1][0] * pr + pieces[-1][1])

    right1_copy = pltpu.make_async_remote_copy(
        src_ref=right1_own, dst_ref=right1_mate, send_sem=m_send, recv_sem=m_recv,
        device_id=at(r, c, mate), device_id_type=MESH,
    )
    right1_copy.start()
    for p in range(pc):
        right1_full[:, pl.ds(col_start(ch, p), 8), :] = right1_own[p].astype(F32).reshape(rb, 8, 128)
    right1_copy.wait_recv()
    for p in range(pc):
        right1_full[:, pl.ds(col_start(mate, p), 8), :] = right1_mate[p].astype(F32).reshape(rb, 8, 128)

    def part1_copy(index, row, core, p):
        return pltpu.make_async_remote_copy(
            src_ref=part1_send.at[index, core, p], dst_ref=part1_got.at[r, p], send_sem=p1_send.at[index, core, p],
            recv_sem=p1_recv.at[r, p], device_id=at(row, c, core), device_id_type=MESH,
        )

    def each_part1(index, row, p, act):
        for core in range(2):
            stays = jnp.logical_and(row == r, ch == core)

            @pl.when(jnp.logical_not(stays))
            def _():
                act(part1_copy(index, row, core, p))

    for d in range(n_col):
        col = lax.rem(c + d, n_col)
        for off in range(q):
            row = (2 * col + ch) * q + off
            index = d * q + off
            for p in range(pr):
                piece = off * pr + p
                if d:
                    left1_copy(d, col, piece).wait_recv()
                left1_full[...] = left1_got[col, piece].astype(F32).reshape(rb, 8, 128)
                for core in range(2):
                    sums = triangle(
                        lambda k, i: left1_full[k, i:i + 1, :],
                        lambda k: right1_full[k, core * cb:(core + 1) * cb, :],
                        rb, cb, 8,
                    )
                    block = jnp.stack([total.reshape(pc, 8, 128) for total in sums], axis=1)
                    part1_send[index, core, p] = block.reshape(cb * 8, 128).astype(BF16)
                each_part1(index, row, p, lambda copy: copy.start())

                @pl.when(row == r)
                def _():
                    pltpu.make_async_copy(
                        part1_send.at[index, ch, p], part1_got.at[r, p], p1_recv.at[r, p]
                    ).start()

    def out_copy(p):
        there = out_ref.at[p * 8:(p + 1) * 8, pl.ds(mine, cb), :]
        return pltpu.make_async_remote_copy(
            src_ref=there, dst_ref=there, send_sem=o_send.at[p],
            recv_sem=o_recv.at[p], device_id=at(r, c, mate), device_id_type=MESH,
        )

    for p in range(pr):
        values = jnp.zeros((cb * 8, 128), F32)
        for row in range(n_row):
            pltpu.make_async_copy(part1_send.at[0, 0, p], part1_got.at[row, p], p1_recv.at[row, p]).wait()
            values += part1_got[row, p].astype(F32)
        update = grown(values, 1)
        for piece in range(pc):
            rows = slice(p * 64, (p + 1) * 64)
            done = cells[piece, rows, :] + gating[piece, rows, :] * update[piece * 64:(piece + 1) * 64]
            out_ref[p * 8:(p + 1) * 8, pl.ds(col_start(ch, piece), 8), :] = done.reshape(8, 8, 128)
        out_copy(p).start()

    for p in range(pr):
        for d in range(1, n_row):
            right_copy(lax.rem(r + d, n_row), aim, d, p).wait_send()

        @pl.when(aim != ch)
        def _():
            right_copy(r, mate, 0, p).wait_send()

    left_copy.wait_send()
    right1_copy.wait_send()
    for d in range(1, n_col):
        for piece in range(pc):
            part0_copy(d, piece).wait_send()
            left1_copy(d, c, piece).wait_send()
    for d in range(n_col):
        for off in range(q):
            row = (2 * lax.rem(c + d, n_col) + ch) * q + off
            for p in range(pr):
                each_part1(d * q + off, row, p, lambda copy: copy.wait_send())
    for p in range(pr):
        out_copy(p).wait()


def on_device(n_row, n_col, pair_state, input_weights, gate_weights, output_weights):
    rb, cols, channels = pair_state.shape
    cb = cols // 2
    q = cb // rb
    pr, pc = rb // 8, cb // 8
    w_in = input_weights.reshape(2, channels, 2, 2 * channels).transpose(0, 2, 1, 3)
    vmem = pl.BlockSpec(memory_space=pltpu.VMEM)
    dma = pltpu.SemaphoreType.DMA
    slots = n_row // 2

    def wide(*shape):
        return pltpu.VMEM((*shape, channels), F32)

    def narrow(*shape):
        return pltpu.VMEM((*shape, channels), BF16)

    scratch = [
        wide(pc, rb * 8), wide(cb * 8), wide(pc, rb * 8), wide(pc, rb * 8),
        narrow(pc, rb * 8), narrow(pc, rb * 8), wide(rb, 2 * cb),
        narrow(pr, cb * 8), narrow(slots, 2, pr, cb * 8), wide(2 * cb, 8),
        narrow(n_col - 1, pc, rb * 8), narrow(n_col - 1, pc, rb * 8),
        narrow(n_col, pc, rb * 8), wide(rb, 8), narrow(pc, rb * 8), narrow(pc, rb * 8), wide(rb, 2 * cb),
        narrow(n_col * q, 2, pr, cb * 8), narrow(n_row, pr, cb * 8),
        dma, dma, dma((n_row, pr)), dma((slots, 2, pr)), dma((n_col - 1, pc)), dma((n_col - 1, pc)),
        dma((n_col - 1, pc)), dma((n_col, pc)), dma, dma, dma((n_col * q, 2, pr)), dma((n_row, pr)),
        dma((pr,)), dma((pr,)),
    ]
    return pl.pallas_call(
        functools.partial(kernel, n_row, n_col),
        out_shape=jax.ShapeDtypeStruct(pair_state.shape, F32),
        in_specs=[vmem] * 4,
        out_specs=vmem,
        scratch_shapes=scratch,
        compiler_params=pltpu.CompilerParams(
            collective_id=0, has_side_effects=True, vmem_limit_bytes=50 * 1024 * 1024
        ),
    )(pair_state, w_in, gate_weights, output_weights)


def solution(mesh):
    placed = (P(("parts", "row"), "col", None), P(), P(), P())
    return jax.shard_map(
        functools.partial(on_device, mesh.shape["row"], mesh.shape["col"]),
        mesh=mesh,
        in_specs=placed,
        out_specs=P(("parts", "row"), "col", None),
        check_vma=False,
    )
```

```python
import functools

import jax
import jax.numpy as jnp
from jax import lax
from jax.experimental import pallas as pl
from jax.experimental.pallas import tpu as pltpu
from jax.sharding import PartitionSpec as P

EPSILON = 1e-05
MESH = pl.DeviceIdType.MESH
BF16, F32 = jnp.bfloat16, jnp.float32


def normalize(values):
    average = jnp.mean(values, axis=-1, keepdims=True)
    centered = values - average
    variance = jnp.mean(centered * centered, axis=-1, keepdims=True)
    return centered * lax.rsqrt(variance + EPSILON)


def sigmoid(v):
    return jax.nn.sigmoid(v)


def triangle(left_row, right_slab, depth, columns, block):
    def step(k, sums):
        right = right_slab(k)
        return tuple(sums[i] + left_row(k, i) * right for i in range(block))

    zero = jnp.zeros((columns, 128), F32)
    return lax.fori_loop(0, depth, step, (zero,) * block, unroll=4)


def kernel(
    n_row, n_col, state_ref, w_in_ref, w_gate_ref, w_out_ref, out_ref,
    cells, turned, gating, mixed0,
    left_own, left_mate, left_full, right_own, right_got, right_full,
    part0_send, part0_got,
    left1_got, left1_full, right1_own, right1_mate, right1_full, part1_send, part1_got, merge_got, fresh,
    l_send, l_recv, r_send, r_recv, f_send, g_send, g_recv, p0_send, p0_recv,
    l1_send, l1_recv, m_send, m_recv, p1_send, p1_recv, o_send, o_recv,
):
    r, c, ch = lax.axis_index("row"), lax.axis_index("col"), lax.axis_index("chan")
    mate = 1 - ch
    rb = state_ref.shape[0]
    cb = state_ref.shape[1] // 2
    q = cb // rb
    pr, pc = rb // 8, cb // 8
    mine = pl.multiple_of(ch * cb, 8)

    def at(row, col, chan):
        return {"row": row, "col": col, "chan": chan}

    def col_start(core, piece):
        return pl.multiple_of(core * cb + piece * 8, 8)

    barrier = pltpu.get_barrier_semaphore()
    greeted = 0
    for dr in range(n_row):
        for dch in range(2):
            if dr or dch:
                pl.semaphore_signal(
                    barrier, inc=1, device_id=at(lax.rem(r + dr, n_row), c, lax.rem(ch + dch, 2)), device_id_type=MESH
                )
                greeted += 1
    for dc in range(1, n_col):
        pl.semaphore_signal(barrier, inc=1, device_id=at(r, lax.rem(c + dc, n_col), ch), device_id_type=MESH)
        greeted += 1

    def panel(normed, u, side):
        both = jnp.dot(normed, w_in_ref[u, side], preferred_element_type=F32)
        return (sigmoid(both[:, :128]) * both[:, 128:]).astype(BF16)

    def gate(normed, u):
        return sigmoid(jnp.dot(normed, w_gate_ref[u], preferred_element_type=F32))

    def grown(values, u):
        return jnp.dot(normalize(values).astype(BF16), w_out_ref[u], preferred_element_type=F32)

    for p in range(pc):
        cells[p] = state_ref[:, pl.ds(col_start(ch, p), 8), :].reshape(rb * 8, 128)

    aim = lax.rem(r // q, 2)
    slot = (r // q) // 2 * q + lax.rem(r, q)

    def right_copy(row, chan, index, p):
        return pltpu.make_async_remote_copy(
            src_ref=right_own.at[p], dst_ref=right_got.at[slot, ch, p], send_sem=r_send.at[index, p],
            recv_sem=r_recv.at[slot, ch, p], device_id=at(row, c, chan), device_id_type=MESH,
        )

    last = n_row - 1
    relays = n_row >= 4
    merges = False

    def right_sends(p, act):
        for d in sorted(range(1, n_row), key=lambda d: abs(2 * d - n_row)):
            row = lax.rem(r + d, n_row)
            if relays and d in (1, last):

                @pl.when(r != (last if d == 1 else 0))
                def _():
                    act(right_copy(row, aim, d, p))
            else:
                act(right_copy(row, aim, d, p))

    def relay_copy(source, core, p, row):
        return pltpu.make_async_remote_copy(
            src_ref=right_got.at[source, core, p], dst_ref=right_got.at[source, core, p], send_sem=f_send.at[core, p],
            recv_sem=r_recv.at[source, core, p], device_id=at(row, c, ch), device_id_type=MESH,
        )

    for p in range(pr):
        for k in range(cb):
            turned[k * 8:(k + 1) * 8, :] = cells[k // 8, pl.ds(p * 64 + k % 8, 8, stride=8), :]
        right_own[p] = panel(normalize(turned[...]).astype(BF16), 0, 1)
        if p == 0:
            pl.semaphore_wait(barrier, greeted)
        right_sends(p, lambda copy: copy.start())

        @pl.when(aim != ch)
        def _():
            right_copy(r, mate, 0, p).start()

        @pl.when(aim == ch)
        def _():
            pltpu.make_async_copy(right_own.at[p], right_got.at[slot, ch, p], r_recv.at[slot, ch, p]).start()

    for p in range(pc):
        normed = normalize(cells[p]).astype(BF16)
        left_own[p] = panel(normed, 0, 0)
        gating[p] = gate(normed, 0)
    left_copy = pltpu.make_async_remote_copy(
        src_ref=left_own, dst_ref=left_mate, send_sem=l_send, recv_sem=l_recv,
        device_id=at(r, c, mate), device_id_type=MESH,
    )
    left_copy.start()
    for p in range(pc):
        left_full[:, pl.ds(col_start(ch, p), 8), :] = left_own[p].astype(F32).reshape(rb, 8, 128)
    left_copy.wait_recv()
    for p in range(pc):
        left_full[:, pl.ds(col_start(mate, p), 8), :] = left_mate[p].astype(F32).reshape(rb, 8, 128)

    def part0_copy(d, piece):
        return pltpu.make_async_remote_copy(
            src_ref=part0_send.at[d - 1, piece], dst_ref=part0_got.at[d - 1, piece], send_sem=p0_send.at[d - 1, piece],
            recv_sem=p0_recv.at[d - 1, piece], device_id=at(r, lax.rem(c + d, n_col), ch), device_id_type=MESH,
        )

    def left1_copy(d, t, piece):
        return pltpu.make_async_remote_copy(
            src_ref=left1_got.at[t, piece], dst_ref=left1_got.at[t, piece], send_sem=l1_send.at[d - 1, piece],
            recv_sem=l1_recv.at[t, piece], device_id=at(r, lax.rem(c + d, n_col), ch), device_id_type=MESH,
        )

    def conclude(piece):
        values = mixed0[piece]
        for d in range(1, n_col):
            part0_copy(d, piece).wait_recv()
            values += part0_got[d - 1, piece].astype(F32)
        state = cells[piece] + gating[piece] * grown(values, 0)
        cells[piece] = state
        normed = normalize(state).astype(BF16)
        left1_got[c, piece] = panel(normed, 1, 0)
        for d in range(1, n_col):
            left1_copy(d, c, piece).start()
        right1_own[piece] = panel(normed, 1, 1)
        gating[piece] = gate(normed, 1)

    pieces = [(off, p) for p in range(pr) for off in range(q)]
    for number, (off, p) in enumerate(pieces):
        piece = off * pr + p
        for d in range(1, n_col + 1):
            source = lax.rem(c + d, n_col) * q + off
            for core in range(2):
                pltpu.make_async_copy(
                    right_own.at[p], right_got.at[source, core, p], r_recv.at[source, core, p]
                ).wait()
                if relays:
                    row = (2 * lax.rem(c + d, n_col) + ch) * q + off

                    @pl.when(jnp.logical_and(row == 0, r == last - 1))
                    def _():
                        relay_copy(source, core, p, last).start()

                    @pl.when(jnp.logical_and(row == last, r == 1))
                    def _():
                        relay_copy(source, core, p, 0).start()

                right_full[core * cb:(core + 1) * cb] = right_got[source, core, p].astype(F32).reshape(cb, 8, 128)
            sums = triangle(
                lambda k, i: left_full[i, pl.ds(k, 1), :], lambda k: right_full[k], 2 * cb, 8, rb
            )
            if d < n_col:
                part0_send[d - 1, piece] = jnp.stack(sums).reshape(rb * 8, 128).astype(BF16)
                part0_copy(d, piece).start()
            else:
                mixed0[piece] = jnp.stack(sums).reshape(rb * 8, 128)
        if number:
            before = pieces[number - 1]
            conclude(before[0] * pr + before[1])
    conclude(pieces[-1][0] * pr + pieces[-1][1])

    right1_copy = pltpu.make_async_remote_copy(
        src_ref=right1_own, dst_ref=right1_mate, send_sem=m_send, recv_sem=m_recv,
        device_id=at(r, c, mate), device_id_type=MESH,
    )
    right1_copy.start()
    for p in range(pc):
        right1_full[:, pl.ds(col_start(ch, p), 8), :] = right1_own[p].astype(F32).reshape(rb, 8, 128)
    right1_copy.wait_recv()
    for p in range(pc):
        right1_full[:, pl.ds(col_start(mate, p), 8), :] = right1_mate[p].astype(F32).reshape(rb, 8, 128)

    def part1_copy(index, row, core, p):
        return pltpu.make_async_remote_copy(
            src_ref=part1_send.at[index, p, core], dst_ref=part1_got.at[r, p], send_sem=p1_send.at[index, p, core],
            recv_sem=p1_recv.at[r, p], device_id=at(row, c, core), device_id_type=MESH,
        )

    def each_part1(index, row, p, act):
        for core in range(2):
            stays = jnp.logical_and(row == r, ch == core)

            @pl.when(jnp.logical_not(stays))
            def _():
                act(part1_copy(index, row, core, p))

    def merge_copy(index, row, p):
        return pltpu.make_async_remote_copy(
            src_ref=part1_send.at[index, p], dst_ref=merge_got.at[p], send_sem=g_send.at[p],
            recv_sem=g_recv.at[p], device_id=at(row, c, ch), device_id_type=MESH,
        )

    def roles(row):
        if not merges:
            return False, False
        first, final = row == 0, row == last
        gives = jnp.logical_or(jnp.logical_and(final, r == 0), jnp.logical_and(first, r == last))
        adds = jnp.logical_or(jnp.logical_and(final, r == 1), jnp.logical_and(first, r == last - 1))
        return gives, adds

    helper = jnp.where(r == 0, 1, last - 1)

    for d in range(n_col):
        col = lax.rem(c + d, n_col)
        for off in range(q):
            row = (2 * col + ch) * q + off
            gives, adds = roles(row)
            index = d * q + off
            for p in range(pr):
                piece = off * pr + p
                if d:
                    left1_copy(d, col, piece).wait_recv()
                left1_full[...] = left1_got[col, piece].astype(F32).reshape(rb, 8, 128)
                for core in range(2):
                    sums = triangle(
                        lambda k, i: left1_full[k, i:i + 1, :],
                        lambda k: right1_full[k, core * cb:(core + 1) * cb, :],
                        rb, cb, 8,
                    )
                    block = jnp.stack([total.reshape(pc, 8, 128) for total in sums], axis=1)
                    if merges:
                        fresh[core] = block.reshape(cb * 8, 128)
                    part1_send[index, p, core] = block.reshape(cb * 8, 128).astype(BF16)
                if merges:

                    @pl.when(adds)
                    def _():
                        merge_copy(index, helper, p).wait_recv()
                        part1_send[index, p] = (fresh[...] + merge_got[p].astype(F32)).astype(BF16)

                    @pl.when(gives)
                    def _():
                        merge_copy(index, helper, p).start()

                    @pl.when(jnp.logical_not(gives))
                    def _():
                        each_part1(index, row, p, lambda copy: copy.start())
                else:
                    each_part1(index, row, p, lambda copy: copy.start())

                @pl.when(row == r)
                def _():
                    pltpu.make_async_copy(
                        part1_send.at[index, p, ch], part1_got.at[r, p], p1_recv.at[r, p]
                    ).start()

    def out_copy(p):
        there = out_ref.at[p * 8:(p + 1) * 8, pl.ds(mine, cb), :]
        return pltpu.make_async_remote_copy(
            src_ref=there, dst_ref=there, send_sem=o_send.at[p],
            recv_sem=o_recv.at[p], device_id=at(r, c, mate), device_id_type=MESH,
        )

    for p in range(pr):
        turned[...] = jnp.zeros((cb * 8, 128), F32)

        def collect(row):
            pltpu.make_async_copy(part1_send.at[0, p, 0], part1_got.at[row, p], p1_recv.at[row, p]).wait()
            turned[...] += part1_got[row, p].astype(F32)

        for row in range(n_row):
            if merges and row in (0, last):
                pl.when(r != last - row)(functools.partial(collect, row))
            else:
                collect(row)
        update = grown(turned[...], 1)
        for piece in range(pc):
            rows = slice(p * 64, (p + 1) * 64)
            done = cells[piece, rows, :] + gating[piece, rows, :] * update[piece * 64:(piece + 1) * 64]
            out_ref[p * 8:(p + 1) * 8, pl.ds(col_start(ch, piece), 8), :] = done.reshape(8, 8, 128)
        out_copy(p).start()

    for p in range(pr):
        right_sends(p, lambda copy: copy.wait_send())
        if relays:
            for core in range(2):

                @pl.when(jnp.logical_and(ch == 0, r == last - 1))
                def _():
                    relay_copy(0, core, p, last).wait_send()

                @pl.when(jnp.logical_and(ch == 1, r == 1))
                def _():
                    relay_copy(n_col * q - 1, core, p, 0).wait_send()

        @pl.when(aim != ch)
        def _():
            right_copy(r, mate, 0, p).wait_send()

    left_copy.wait_send()
    right1_copy.wait_send()
    for d in range(1, n_col):
        for piece in range(pc):
            part0_copy(d, piece).wait_send()
            left1_copy(d, c, piece).wait_send()
    for d in range(n_col):
        for off in range(q):
            row = (2 * lax.rem(c + d, n_col) + ch) * q + off
            gives, _ = roles(row)
            for p in range(pr):
                if merges:

                    @pl.when(gives)
                    def _():
                        merge_copy(d * q + off, helper, p).wait_send()

                    @pl.when(jnp.logical_not(gives))
                    def _():
                        each_part1(d * q + off, row, p, lambda copy: copy.wait_send())
                else:
                    each_part1(d * q + off, row, p, lambda copy: copy.wait_send())
    for p in range(pr):
        out_copy(p).wait()


def on_device(n_row, n_col, pair_state, input_weights, gate_weights, output_weights):
    rb, cols, channels = pair_state.shape
    cb = cols // 2
    q = cb // rb
    pr, pc = rb // 8, cb // 8
    w_in = input_weights.reshape(2, channels, 2, 2 * channels).transpose(0, 2, 1, 3)
    vmem = pl.BlockSpec(memory_space=pltpu.VMEM)
    dma = pltpu.SemaphoreType.DMA
    slots = n_row // 2

    def wide(*shape):
        return pltpu.VMEM((*shape, channels), F32)

    def narrow(*shape):
        return pltpu.VMEM((*shape, channels), BF16)

    scratch = [
        wide(pc, rb * 8), wide(cb * 8), wide(pc, rb * 8), wide(pc, rb * 8),
        narrow(pc, rb * 8), narrow(pc, rb * 8), wide(rb, 2 * cb),
        narrow(pr, cb * 8), narrow(slots, 2, pr, cb * 8), wide(2 * cb, 8),
        narrow(n_col - 1, pc, rb * 8), narrow(n_col - 1, pc, rb * 8),
        narrow(n_col, pc, rb * 8), wide(rb, 8), narrow(pc, rb * 8), narrow(pc, rb * 8), wide(rb, 2 * cb),
        narrow(n_col * q, pr, 2, cb * 8), narrow(n_row, pr, cb * 8), narrow(pr, 2, cb * 8), wide(2, cb * 8),
        dma, dma, dma((n_row, pr)), dma((slots, 2, pr)), dma((2, pr)), dma((pr,)), dma((pr,)), dma((n_col - 1, pc)), dma((n_col - 1, pc)),
        dma((n_col - 1, pc)), dma((n_col, pc)), dma, dma, dma((n_col * q, pr, 2)), dma((n_row, pr)),
        dma((pr,)), dma((pr,)),
    ]
    return pl.pallas_call(
        functools.partial(kernel, n_row, n_col),
        out_shape=jax.ShapeDtypeStruct(pair_state.shape, F32),
        in_specs=[vmem] * 4,
        out_specs=vmem,
        scratch_shapes=scratch,
        compiler_params=pltpu.CompilerParams(
            collective_id=0, has_side_effects=True, vmem_limit_bytes=50 * 1024 * 1024
        ),
    )(pair_state, w_in, gate_weights, output_weights)


def solution(mesh):
    placed = (P(("parts", "row"), "col", None), P(), P(), P())
    return jax.shard_map(
        functools.partial(on_device, mesh.shape["row"], mesh.shape["col"]),
        mesh=mesh,
        in_specs=placed,
        out_specs=P(("parts", "row"), "col", None),
        check_vma=False,
    )
```

```python
import functools

import jax
import jax.numpy as jnp
from jax import lax
from jax.experimental import pallas as pl
from jax.experimental.pallas import tpu as pltpu
from jax.sharding import PartitionSpec as P

EPSILON = 1e-05
MESH = pl.DeviceIdType.MESH
BF16, F32 = jnp.bfloat16, jnp.float32


def normalize(values):
    average = jnp.mean(values, axis=-1, keepdims=True)
    centered = values - average
    variance = jnp.mean(centered * centered, axis=-1, keepdims=True)
    return centered * lax.rsqrt(variance + EPSILON)


def sigmoid(v):
    return jax.nn.sigmoid(v)


def triangle(left_row, right_slab, depth, columns, block):
    def step(k, sums):
        right = right_slab(k)
        return tuple(sums[i] + left_row(k, i) * right for i in range(block))

    zero = jnp.zeros((columns, 128), F32)
    return lax.fori_loop(0, depth, step, (zero,) * block, unroll=4)


def kernel(
    n_row, n_col, state_ref, w_in_ref, w_gate_ref, w_out_ref, out_ref,
    cells, turned, gating, mixed0,
    left_own, left_mate, left_full, right_own, right_got, right_full,
    part0_send, part0_got,
    left1_got, left1_full, right1_own, right1_mate, right1_full, part1_send, part1_got, merge_got, fresh,
    l_send, l_recv, r_send, r_recv, f_send, g_send, g_recv, p0_send, p0_recv,
    l1_send, l1_recv, m_send, m_recv, p1_send, p1_recv, o_send, o_recv,
):
    r, c, ch = lax.axis_index("row"), lax.axis_index("col"), lax.axis_index("chan")
    mate = 1 - ch
    rb = state_ref.shape[0]
    cb = state_ref.shape[1] // 2
    q = cb // rb
    pr, pc = rb // 8, cb // 8
    mine = pl.multiple_of(ch * cb, 8)

    def at(row, col, chan):
        return {"row": row, "col": col, "chan": chan}

    def col_start(core, piece):
        return pl.multiple_of(core * cb + piece * 8, 8)

    barrier = pltpu.get_barrier_semaphore()
    greeted = 0
    for dr in range(n_row):
        for dch in range(2):
            if dr or dch:
                pl.semaphore_signal(
                    barrier, inc=1, device_id=at(lax.rem(r + dr, n_row), c, lax.rem(ch + dch, 2)), device_id_type=MESH
                )
                greeted += 1
    for dc in range(1, n_col):
        pl.semaphore_signal(barrier, inc=1, device_id=at(r, lax.rem(c + dc, n_col), ch), device_id_type=MESH)
        greeted += 1

    def panel(normed, u, side):
        both = jnp.dot(normed, w_in_ref[u, side], preferred_element_type=F32)
        return (sigmoid(both[:, :128]) * both[:, 128:]).astype(BF16)

    def gate(normed, u):
        return sigmoid(jnp.dot(normed, w_gate_ref[u], preferred_element_type=F32))

    def grown(values, u):
        return jnp.dot(normalize(values).astype(BF16), w_out_ref[u], preferred_element_type=F32)

    for p in range(pc):
        cells[p] = state_ref[:, pl.ds(col_start(ch, p), 8), :].reshape(rb * 8, 128)

    aim = lax.rem(r // q, 2)
    slot = (r // q) // 2 * q + lax.rem(r, q)

    def right_copy(row, chan, index, p):
        return pltpu.make_async_remote_copy(
            src_ref=right_own.at[p], dst_ref=right_got.at[slot, ch, p], send_sem=r_send.at[index, p],
            recv_sem=r_recv.at[slot, ch, p], device_id=at(row, c, chan), device_id_type=MESH,
        )

    last = n_row - 1
    relays = n_row >= 4
    merges = False

    def right_sends(p, act):
        for d in sorted(range(1, n_row), key=lambda d: abs(2 * d - n_row)):
            row = lax.rem(r + d, n_row)
            if relays and d in (1, last):

                @pl.when(r != (last if d == 1 else 0))
                def _():
                    act(right_copy(row, aim, d, p))
            else:
                act(right_copy(row, aim, d, p))

    def relay_copy(source, core, p, row):
        return pltpu.make_async_remote_copy(
            src_ref=right_got.at[source, core, p], dst_ref=right_got.at[source, core, p], send_sem=f_send.at[core, p],
            recv_sem=r_recv.at[source, core, p], device_id=at(row, c, ch), device_id_type=MESH,
        )

    for p in range(pr):
        for k in range(cb):
            turned[k * 8:(k + 1) * 8, :] = cells[k // 8, pl.ds(p * 64 + k % 8, 8, stride=8), :]
        right_own[p] = panel(normalize(turned[...]).astype(BF16), 0, 1)
        if p == 0:
            pl.semaphore_wait(barrier, greeted)
        right_sends(p, lambda copy: copy.start())

        @pl.when(aim != ch)
        def _():
            right_copy(r, mate, 0, p).start()

        @pl.when(aim == ch)
        def _():
            pltpu.make_async_copy(right_own.at[p], right_got.at[slot, ch, p], r_recv.at[slot, ch, p]).start()

    for p in range(pc):
        normed = normalize(cells[p]).astype(BF16)
        left_own[p] = panel(normed, 0, 0)
        gating[p] = gate(normed, 0)
    left_copy = pltpu.make_async_remote_copy(
        src_ref=left_own, dst_ref=left_mate, send_sem=l_send, recv_sem=l_recv,
        device_id=at(r, c, mate), device_id_type=MESH,
    )
    left_copy.start()
    for p in range(pc):
        left_full[:, pl.ds(col_start(ch, p), 8), :] = left_own[p].astype(F32).reshape(rb, 8, 128)
    left_copy.wait_recv()
    for p in range(pc):
        left_full[:, pl.ds(col_start(mate, p), 8), :] = left_mate[p].astype(F32).reshape(rb, 8, 128)

    def part0_copy(d, piece):
        return pltpu.make_async_remote_copy(
            src_ref=part0_send.at[d - 1, piece], dst_ref=part0_got.at[d - 1, piece], send_sem=p0_send.at[d - 1, piece],
            recv_sem=p0_recv.at[d - 1, piece], device_id=at(r, lax.rem(c + d, n_col), ch), device_id_type=MESH,
        )

    def left1_copy(d, t, piece):
        return pltpu.make_async_remote_copy(
            src_ref=left1_got.at[t, piece], dst_ref=left1_got.at[t, piece], send_sem=l1_send.at[d - 1, piece],
            recv_sem=l1_recv.at[t, piece], device_id=at(r, lax.rem(c + d, n_col), ch), device_id_type=MESH,
        )

    def right1_copy(piece):
        return pltpu.make_async_remote_copy(
            src_ref=right1_own.at[piece], dst_ref=right1_mate.at[piece], send_sem=m_send.at[piece],
            recv_sem=m_recv.at[piece], device_id=at(r, c, mate), device_id_type=MESH,
        )

    def conclude(piece):
        values = mixed0[piece]
        for d in range(1, n_col):
            part0_copy(d, piece).wait_recv()
            values += part0_got[d - 1, piece].astype(F32)
        state = cells[piece] + gating[piece] * grown(values, 0)
        cells[piece] = state
        normed = normalize(state).astype(BF16)
        left1_got[c, piece] = panel(normed, 1, 0)
        for d in range(1, n_col):
            left1_copy(d, c, piece).start()
        right1_own[piece] = panel(normed, 1, 1)
        right1_copy(piece).start()
        gating[piece] = gate(normed, 1)

    pieces = [(off, p) for p in range(pr) for off in range(q)]
    for number, (off, p) in enumerate(pieces):
        piece = off * pr + p
        for d in range(1, n_col + 1):
            source = lax.rem(c + d, n_col) * q + off
            for core in range(2):
                pltpu.make_async_copy(
                    right_own.at[p], right_got.at[source, core, p], r_recv.at[source, core, p]
                ).wait()
                if relays:
                    row = (2 * lax.rem(c + d, n_col) + ch) * q + off

                    @pl.when(jnp.logical_and(row == 0, r == last - 1))
                    def _():
                        relay_copy(source, core, p, last).start()

                    @pl.when(jnp.logical_and(row == last, r == 1))
                    def _():
                        relay_copy(source, core, p, 0).start()

                right_full[core * cb:(core + 1) * cb] = right_got[source, core, p].astype(F32).reshape(cb, 8, 128)
            sums = triangle(
                lambda k, i: left_full[i, pl.ds(k, 1), :], lambda k: right_full[k], 2 * cb, 8, rb
            )
            if d < n_col:
                part0_send[d - 1, piece] = jnp.stack(sums).reshape(rb * 8, 128).astype(BF16)
                part0_copy(d, piece).start()
            else:
                mixed0[piece] = jnp.stack(sums).reshape(rb * 8, 128)
        if number:
            before = pieces[number - 1]
            conclude(before[0] * pr + before[1])
    conclude(pieces[-1][0] * pr + pieces[-1][1])

    for p in range(pc):
        right1_full[:, pl.ds(col_start(ch, p), 8), :] = right1_own[p].astype(F32).reshape(rb, 8, 128)
    for p in range(pc):
        right1_copy(p).wait_recv()
        right1_full[:, pl.ds(col_start(mate, p), 8), :] = right1_mate[p].astype(F32).reshape(rb, 8, 128)

    def part1_copy(index, row, core, p):
        return pltpu.make_async_remote_copy(
            src_ref=part1_send.at[index, p, core], dst_ref=part1_got.at[r, p], send_sem=p1_send.at[index, p, core],
            recv_sem=p1_recv.at[r, p], device_id=at(row, c, core), device_id_type=MESH,
        )

    def each_part1(index, row, p, act):
        for core in range(2):
            stays = jnp.logical_and(row == r, ch == core)

            @pl.when(jnp.logical_not(stays))
            def _():
                act(part1_copy(index, row, core, p))

    def merge_copy(index, row, p):
        return pltpu.make_async_remote_copy(
            src_ref=part1_send.at[index, p], dst_ref=merge_got.at[p], send_sem=g_send.at[p],
            recv_sem=g_recv.at[p], device_id=at(row, c, ch), device_id_type=MESH,
        )

    def roles(row):
        if not merges:
            return False, False
        first, final = row == 0, row == last
        gives = jnp.logical_or(jnp.logical_and(final, r == 0), jnp.logical_and(first, r == last))
        adds = jnp.logical_or(jnp.logical_and(final, r == 1), jnp.logical_and(first, r == last - 1))
        return gives, adds

    helper = jnp.where(r == 0, 1, last - 1)

    for d in range(n_col):
        col = lax.rem(c + d, n_col)
        for off in range(q):
            row = (2 * col + ch) * q + off
            gives, adds = roles(row)
            index = d * q + off
            for p in range(pr):
                piece = off * pr + p
                if d:
                    left1_copy(d, col, piece).wait_recv()
                left1_full[...] = left1_got[col, piece].astype(F32).reshape(rb, 8, 128)
                for core in range(2):
                    sums = triangle(
                        lambda k, i: left1_full[k, i:i + 1, :],
                        lambda k: right1_full[k, core * cb:(core + 1) * cb, :],
                        rb, cb, 8,
                    )
                    block = jnp.stack([total.reshape(pc, 8, 128) for total in sums], axis=1)
                    if merges:
                        fresh[core] = block.reshape(cb * 8, 128)
                    part1_send[index, p, core] = block.reshape(cb * 8, 128).astype(BF16)
                if merges:

                    @pl.when(adds)
                    def _():
                        merge_copy(index, helper, p).wait_recv()
                        part1_send[index, p] = (fresh[...] + merge_got[p].astype(F32)).astype(BF16)

                    @pl.when(gives)
                    def _():
                        merge_copy(index, helper, p).start()

                    @pl.when(jnp.logical_not(gives))
                    def _():
                        each_part1(index, row, p, lambda copy: copy.start())
                else:
                    each_part1(index, row, p, lambda copy: copy.start())

                @pl.when(row == r)
                def _():
                    pltpu.make_async_copy(
                        part1_send.at[index, p, ch], part1_got.at[r, p], p1_recv.at[r, p]
                    ).start()

    def out_copy(p):
        there = out_ref.at[p * 8:(p + 1) * 8, pl.ds(mine, cb), :]
        return pltpu.make_async_remote_copy(
            src_ref=there, dst_ref=there, send_sem=o_send.at[p],
            recv_sem=o_recv.at[p], device_id=at(r, c, mate), device_id_type=MESH,
        )

    for p in range(pr):
        turned[...] = jnp.zeros((cb * 8, 128), F32)

        def collect(row):
            pltpu.make_async_copy(part1_send.at[0, p, 0], part1_got.at[row, p], p1_recv.at[row, p]).wait()
            turned[...] += part1_got[row, p].astype(F32)

        for row in range(n_row):
            if merges and row in (0, last):
                pl.when(r != last - row)(functools.partial(collect, row))
            else:
                collect(row)
        update = grown(turned[...], 1)
        for piece in range(pc):
            rows = slice(p * 64, (p + 1) * 64)
            done = cells[piece, rows, :] + gating[piece, rows, :] * update[piece * 64:(piece + 1) * 64]
            out_ref[p * 8:(p + 1) * 8, pl.ds(col_start(ch, piece), 8), :] = done.reshape(8, 8, 128)
        out_copy(p).start()

    for p in range(pr):
        right_sends(p, lambda copy: copy.wait_send())
        if relays:
            for core in range(2):

                @pl.when(jnp.logical_and(ch == 0, r == last - 1))
                def _():
                    relay_copy(0, core, p, last).wait_send()

                @pl.when(jnp.logical_and(ch == 1, r == 1))
                def _():
                    relay_copy(n_col * q - 1, core, p, 0).wait_send()

        @pl.when(aim != ch)
        def _():
            right_copy(r, mate, 0, p).wait_send()

    left_copy.wait_send()
    for p in range(pc):
        right1_copy(p).wait_send()
    for d in range(1, n_col):
        for piece in range(pc):
            part0_copy(d, piece).wait_send()
            left1_copy(d, c, piece).wait_send()
    for d in range(n_col):
        for off in range(q):
            row = (2 * lax.rem(c + d, n_col) + ch) * q + off
            gives, _ = roles(row)
            for p in range(pr):
                if merges:

                    @pl.when(gives)
                    def _():
                        merge_copy(d * q + off, helper, p).wait_send()

                    @pl.when(jnp.logical_not(gives))
                    def _():
                        each_part1(d * q + off, row, p, lambda copy: copy.wait_send())
                else:
                    each_part1(d * q + off, row, p, lambda copy: copy.wait_send())
    for p in range(pr):
        out_copy(p).wait()


def on_device(n_row, n_col, pair_state, input_weights, gate_weights, output_weights):
    rb, cols, channels = pair_state.shape
    cb = cols // 2
    q = cb // rb
    pr, pc = rb // 8, cb // 8
    w_in = input_weights.reshape(2, channels, 2, 2 * channels).transpose(0, 2, 1, 3)
    vmem = pl.BlockSpec(memory_space=pltpu.VMEM)
    dma = pltpu.SemaphoreType.DMA
    slots = n_row // 2

    def wide(*shape):
        return pltpu.VMEM((*shape, channels), F32)

    def narrow(*shape):
        return pltpu.VMEM((*shape, channels), BF16)

    scratch = [
        wide(pc, rb * 8), wide(cb * 8), wide(pc, rb * 8), wide(pc, rb * 8),
        narrow(pc, rb * 8), narrow(pc, rb * 8), wide(rb, 2 * cb),
        narrow(pr, cb * 8), narrow(slots, 2, pr, cb * 8), wide(2 * cb, 8),
        narrow(n_col - 1, pc, rb * 8), narrow(n_col - 1, pc, rb * 8),
        narrow(n_col, pc, rb * 8), wide(rb, 8), narrow(pc, rb * 8), narrow(pc, rb * 8), wide(rb, 2 * cb),
        narrow(n_col * q, pr, 2, cb * 8), narrow(n_row, pr, cb * 8), narrow(pr, 2, cb * 8), wide(2, cb * 8),
        dma, dma, dma((n_row, pr)), dma((slots, 2, pr)), dma((2, pr)), dma((pr,)), dma((pr,)), dma((n_col - 1, pc)), dma((n_col - 1, pc)),
        dma((n_col - 1, pc)), dma((n_col, pc)), dma((pc,)), dma((pc,)), dma((n_col * q, pr, 2)), dma((n_row, pr)),
        dma((pr,)), dma((pr,)),
    ]
    return pl.pallas_call(
        functools.partial(kernel, n_row, n_col),
        out_shape=jax.ShapeDtypeStruct(pair_state.shape, F32),
        in_specs=[vmem] * 4,
        out_specs=vmem,
        scratch_shapes=scratch,
        compiler_params=pltpu.CompilerParams(
            collective_id=0, has_side_effects=True, vmem_limit_bytes=50 * 1024 * 1024
        ),
    )(pair_state, w_in, gate_weights, output_weights)


def solution(mesh):
    placed = (P(("parts", "row"), "col", None), P(), P(), P())
    return jax.shard_map(
        functools.partial(on_device, mesh.shape["row"], mesh.shape["col"]),
        mesh=mesh,
        in_specs=placed,
        out_specs=P(("parts", "row"), "col", None),
        check_vma=False,
    )
```
